32 devices in a mesh: dm: 4 (over z), hv: 8 (over y, x, core).
Axes of the slice: x: 2, y: 2, z: 4, core: 2. Of those that a mesh axis runs over, the one named last changes fastest.
Arguments:
- tokens: bfloat16 [512, 16384], P('hv', 'dm'), may hold values from -64 to 64
- gate_weight: bfloat16 [16384, 13312], P('dm', 'hv'), may hold values from -0.046875 to 0.046875
- up_weight: bfloat16 [16384, 13312], P('dm', 'hv'), may hold values from -0.046875 to 0.046875
- down_weight: bfloat16 [13312, 16384], P('hv', 'dm'), may hold values from -0.0546875 to 0.0546875
- norm_gain: float32 [16384], P('dm'), may hold values from 0.1 to 1.9
- unembed: bfloat16 [16384, 32064], P('dm', 'hv'), may hold values from -8 to 8
- gold_ids: int32 [512], replicated, may hold values from 0 to 32063
- option_lengths: int32 [32], replicated, may hold values from 1 to 32, 512 in all
Outputs:
- token_logprob: float32 [512], replicated
- option_score: float32 [32], replicated
The draws below stay inside these ranges and needn't reach their ends.
All inputs are finite; a program needn't handle non-finite values.
Results may differ from the reference program's by a relative error of at most 0.005.
Values may be sent and summed in bfloat16 or wider, within the bound.
No kernel may reach another device: no remote copies, remote signals or barrier semaphores. Data moves between devices by JAX's collectives and lax.ppermute only.
A program may use at most 128 MiB of HBM per device.

```python
import math
import jax
import jax.numpy as jnp
import numpy as np
from jax import lax

D = 16384
FF = 13312
V = 32064
TOKENS = 512
MOST = 32
NOPT = 32


def draw_tokens(key, part):
    first, second, third = jax.random.split(key, 3)
    column = jnp.exp(jnp.arange(D, dtype=jnp.float32) * (math.log(3.0) / D))
    column = column * jnp.exp(jax.random.uniform(second, (D,), jnp.float32, -0.7, 0.7))
    base = jnp.clip(jax.random.normal(first, (TOKENS, D), jnp.float32), -4.0, 4.0)
    rowscale = jnp.exp(jax.random.uniform(third, (TOKENS, 1), jnp.float32, 0.0, math.log(4.0)))
    return (0.5 * base * rowscale * column).astype(jnp.bfloat16)


def draw_unembed(key, part):
    first = jax.random.fold_in(key, 0)
    base = jnp.clip(jax.random.normal(first, (D, V), jnp.float32), -4.0, 4.0)
    values = base * (3.0 / math.sqrt(D))
    return jnp.clip(values, -8.0, 8.0).astype(jnp.bfloat16)


def set_ends(values, own_key, least, high):
    extent = values.shape
    spot = [jax.random.randint(jax.random.fold_in(own_key, axis), (), 0, extent[axis]) for axis in range(len(extent))]
    values = values.at[tuple(spot)].set(least)
    longest = extent.index(max(extent))
    spot[longest] = (spot[longest] + 1) % extent[longest]
    return values.at[tuple(spot)].set(high)


def shard_levels(rng, shape, cuts, least, high):
    def one(position, shards_of):
        heights = jax.random.uniform(jax.random.fold_in(jax.random.fold_in(rng, 6), position), (shards_of,), jnp.float32, least / len(cuts), high / len(cuts))
        return jnp.repeat(jnp.exp(heights), shape[position] // shards_of).reshape((-1,) + (1,) * (len(shape) - position - 1))

    factor_of = one(*cuts[0])
    for cut in cuts[1:]:
        factor_of = factor_of * one(*cut)
    return factor_of


def split_up(count, total, reach, lean):
    loads = [(1 << 20) // math.isqrt(rank ** lean) + 1 for rank in range(2, count + 1)]
    spare, holding = total - reach - (count - 1), [1] * (count - 1)
    while spare > 0:
        candidates = [i for i in range(count - 1) if holding[i] < reach]
        mass, budget = sum([loads[i] for i in candidates]), spare
        for i in candidates:
            extra = min(reach - holding[i], max(1, budget * loads[i] // mass), spare)
            holding[i] = holding[i] + extra
            spare = spare - extra
    return np.array([reach] + holding)


def uneven(own_key, amount, total, most, lean):
    if amount == 2:
        one = jax.random.randint(own_key, (), max(1, total - most), min(most, total - 1) + 1)
        return jnp.stack([one, total - one])
    sizes = jnp.asarray(split_up(amount, total, most, lean), jnp.int32)
    pairs = (amount - 1) // 2
    donor, sink = sizes[1:1 + 2 * pairs:2], sizes[2:2 + 2 * pairs:2]
    margin = jnp.minimum(donor - 1, most - sink)
    passed = jax.random.randint(jax.random.fold_in(own_key, 1), (pairs,), 0, 1 << 20) % (margin + 1)
    sizes = sizes.at[1:1 + 2 * pairs:2].set(donor - passed).at[2:2 + 2 * pairs:2].set(sink + passed)
    return sizes[jax.random.permutation(jax.random.fold_in(own_key, 2), amount)]


def bell_draw(stream_key, extent, scale, most, shards=(), held_as=jnp.bfloat16):
    gain = shard_levels(stream_key, extent, shards, -0.22, 0.18) if shards else 1.0
    array = jax.random.normal(stream_key, extent, jnp.float32) * scale * gain
    return jnp.minimum(jnp.maximum(array, -most), most).astype(held_as)


def setup_inputs(seed: int = 0) -> dict:
    streams_of = jax.random.split(jax.random.key(seed), 9)
    return {
        "tokens": draw_tokens(jax.random.fold_in(streams_of[8], 71), 0),
        "gate_weight": bell_draw(streams_of[1], (D, FF), D ** -0.5, 0.046875, ((0, 4), (1, 8))),
        "up_weight": bell_draw(streams_of[2], (D, FF), D ** -0.5, 0.046875, ((0, 4), (1, 8))),
        "down_weight": bell_draw(streams_of[3], (FF, D), FF ** -0.5, 0.0546875, ((0, 8), (1, 4))),
        "norm_gain": jnp.clip(1.0 + 0.18 * jax.random.normal(streams_of[4], (D,), jnp.float32), 0.1, 1.9),
        "unembed": draw_unembed(jax.random.fold_in(streams_of[8], 71), 0),
        "gold_ids": set_ends(jax.random.randint(streams_of[6], (TOKENS,), 0, V), jax.random.fold_in(streams_of[6], 1), 0, V - 1).astype(jnp.int32),
        "option_lengths": uneven(streams_of[7], NOPT, TOKENS, MOST, 1).astype(jnp.int32),
    }


def reference(tokens, gate_weight, up_weight, down_weight, norm_gain, unembed, gold_ids, option_lengths):
    gate = jnp.dot(tokens, gate_weight, preferred_element_type=jnp.float32)
    up = jnp.dot(tokens, up_weight, preferred_element_type=jnp.float32)
    hidden = (jax.nn.silu(gate) * up).astype(jnp.bfloat16)
    ffn = jnp.dot(hidden, down_weight, preferred_element_type=jnp.float32)
    resid = (tokens.astype(jnp.float32) + ffn).astype(jnp.bfloat16)
    wide = resid.astype(jnp.float32)
    squares = lax.optimization_barrier(jnp.sum(wide * wide, axis=1, keepdims=True))
    normed = (wide * lax.rsqrt(squares / D + 1e-05) * norm_gain).astype(jnp.bfloat16)
    logits = jnp.dot(normed, unembed, preferred_element_type=jnp.float32)
    top = lax.optimization_barrier(jnp.max(logits, axis=1))
    total = lax.optimization_barrier(jnp.sum(jnp.exp(logits - top[:, None]), axis=1))
    gold = jnp.take_along_axis(logits, gold_ids[:, None].astype(jnp.int32), axis=1)[:, 0]
    token_logprob = gold - top - jnp.log(total)
    ends = jnp.cumsum(option_lengths)
    starts = ends - option_lengths
    places = jnp.arange(TOKENS, dtype=jnp.int32)
    member = ((places[None, :] >= starts[:, None]) & (places[None, :] < ends[:, None])).astype(jnp.float32)
    summed = jnp.dot(member, token_logprob, precision=lax.Precision.HIGHEST)
    option_score = summed / option_lengths.astype(jnp.float32)
    return (token_logprob, option_score)
```

```python
import functools

import jax
import jax.numpy as jnp
import numpy as np
from jax import lax
from jax.sharding import PartitionSpec as P

D = 16384
BATCHES = 2
F32 = jnp.float32
BF16 = jnp.bfloat16


def dm_steps(n):
    return [(lambda i, k=k: (i >> k) & 1, lambda i, k=k: i ^ (1 << k)) for k in range(n.bit_length() - 1)]


def hv_steps(n):
    if n != 8:
        return dm_steps(n)
    return [
        (lambda i: i & 1, lambda i: i ^ 1),
        (lambda i: (i >> (1 + (i & 1))) & 1, lambda i: i ^ (2 << (i & 1))),
        (lambda i: (i >> (2 - (i & 1))) & 1, lambda i: i ^ (4 >> (i & 1))),
    ]


def places(steps, n):
    out = []
    for i in range(n):
        place = 0
        for bit, _ in steps:
            place = 2 * place + bit(i)
        out.append(place)
    return np.array(out)


def scatter(array, axis, steps, n):
    index = lax.axis_index(axis)
    for bit, partner in steps:
        half = array.shape[0] // 2
        mine = bit(index)
        sent = lax.dynamic_slice_in_dim(array, (1 - mine) * half, half, 0)
        got = lax.ppermute(sent, axis, [(i, partner(i)) for i in range(n)])
        kept = lax.dynamic_slice_in_dim(array, mine * half, half, 0)
        array = (kept.astype(F32) + got.astype(F32)).astype(BF16)
    return array


def gather(array, axis, steps, n):
    index = lax.axis_index(axis)
    for bit, partner in reversed(steps):
        got = lax.ppermute(array, axis, [(i, partner(i)) for i in range(n)])
        low = bit(index) == 0
        array = jnp.concatenate([jnp.where(low, array, got), jnp.where(low, got, array)], axis=0)
    return array


def per_device(
    tokens, gate_weight, up_weight, down_weight, norm_gain, unembed, gold_ids, option_lengths, *, n_dm, n_hv
):
    width = gate_weight.shape[1]
    own = tokens.shape[0] // BATCHES
    rows = own * n_hv
    over_dm, over_hv = dm_steps(n_dm), hv_steps(n_hv)
    dm_place, hv_place = places(over_dm, n_dm), places(over_hv, n_hv)
    dm, hv = lax.axis_index("dm"), lax.axis_index("hv")
    spot = jnp.asarray(dm_place)[dm]
    share = rows // n_dm
    golds = gold_ids.reshape(n_hv, BATCHES, own)[np.argsort(hv_place)]
    offset = hv * unembed.shape[1]
    stats = []
    for b in range(BATCHES):
        mine = tokens[b * own : (b + 1) * own]
        piece = gather(mine, "hv", over_hv, n_hv)
        gate = jnp.dot(piece, gate_weight, preferred_element_type=F32).astype(BF16)
        up = jnp.dot(piece, up_weight, preferred_element_type=F32).astype(BF16)
        summed = scatter(jnp.concatenate([gate, up], axis=1), "dm", over_dm, n_dm).astype(F32)
        hidden = (jax.nn.silu(summed[:, :width]) * summed[:, width:]).astype(BF16)
        hidden = gather(hidden, "dm", over_dm, n_dm)
        ffn = jnp.dot(hidden, down_weight, preferred_element_type=F32).astype(BF16)
        ffn = scatter(ffn, "hv", over_hv, n_hv)
        resid = (mine.astype(F32) + ffn.astype(F32)).astype(BF16)
        whole = gather(resid, "hv", over_hv, n_hv)
        wide = whole.astype(F32)
        squares = lax.psum(jnp.sum(wide * wide, axis=1), "dm")
        scaled = (wide * norm_gain).astype(BF16)
        partial = jnp.dot(scaled, unembed, preferred_element_type=F32).astype(BF16)
        part = scatter(partial, "dm", over_dm, n_dm)
        scale = lax.rsqrt(lax.dynamic_slice_in_dim(squares, spot * share, share, 0) / D + 1e-05)
        logits = part.astype(F32) * scale[:, None]
        gold = lax.dynamic_slice_in_dim(golds[:, b].reshape(-1), spot * share, share, 0)
        hit = lax.broadcasted_iota(jnp.int32, logits.shape, 1) + offset == gold[:, None]
        gold_part = jnp.sum(jnp.where(hit, logits, 0.0), axis=1)
        top = jnp.max(logits, axis=1)
        total = jnp.sum(jnp.exp(logits - top[:, None]), axis=1)
        stats.append(jnp.stack([top, total, gold_part]))
    stats = lax.all_gather(jnp.stack(stats), "hv", axis=0)
    top = jnp.max(stats[:, :, 0], axis=0)
    total = jnp.sum(stats[:, :, 1] * jnp.exp(stats[:, :, 0] - top), axis=0)
    gold = jnp.sum(stats[:, :, 2], axis=0)
    logprob = lax.all_gather(gold - top - jnp.log(total), "dm", axis=0)
    logprob = logprob[np.argsort(dm_place)]
    logprob = logprob.transpose(1, 0, 2).reshape(BATCHES, n_hv, own)
    token_logprob = logprob[:, hv_place].transpose(1, 0, 2).reshape(-1)
    ends = jnp.cumsum(option_lengths)
    starts = ends - option_lengths
    spots = jnp.arange(token_logprob.shape[0], dtype=jnp.int32)
    member = ((spots[None, :] >= starts[:, None]) & (spots[None, :] < ends[:, None])).astype(F32)
    option_sums = jnp.dot(member, token_logprob, precision=lax.Precision.HIGHEST)
    option_score = option_sums / option_lengths.astype(F32)
    return (token_logprob, option_score)


def solution(mesh):
    placed = (
        P("hv", "dm"),
        P("dm", "hv"),
        P("dm", "hv"),
        P("hv", "dm"),
        P("dm"),
        P("dm", "hv"),
        P(),
        P(),
    )
    body = functools.partial(per_device, n_dm=mesh.shape["dm"], n_hv=mesh.shape["hv"])
    return jax.shard_map(
        body, mesh=mesh, in_specs=placed, out_specs=(P(), P()), check_vma=False
    )
```

```python
import functools

import jax
import jax.numpy as jnp
from jax import lax
from jax.experimental import pallas as pl
from jax.experimental.pallas import tpu as pltpu
from jax.sharding import PartitionSpec as P

D = 16384
DOWN_CHUNKS = 2
VOCAB_TILE = 1024
F32 = jnp.float32
BF16 = jnp.bfloat16
MIB = 1 << 20
VMEM = pl.BlockSpec(memory_space=pltpu.VMEM)
SMEM = pl.BlockSpec(memory_space=pltpu.SMEM)
ANY = pl.BlockSpec(memory_space=pl.ANY)
DM_FIRST, DM_LAST, CORE, OFFSET = range(4)


def run(scalars, body, outs, arrays, after=None):
    ahead = [] if after is None else [after]

    def kernel(scalars, *refs):
        body(scalars, *refs[: len(arrays)], *refs[len(arrays) + len(ahead) :])

    return pl.pallas_call(
        kernel,
        out_shape=[jax.ShapeDtypeStruct(*out) for out in outs],
        in_specs=[SMEM, *[VMEM] * len(arrays), *[ANY] * len(ahead)],
        out_specs=[VMEM] * len(outs),
        compiler_params=pltpu.CompilerParams(vmem_limit_bytes=12 * MIB),
        cost_estimate=pl.CostEstimate(
            flops=0, bytes_accessed=2 * sum(a.size * a.dtype.itemsize for a in arrays), transcendentals=0
        ),
    )(scalars, *arrays, *ahead)


def tie(array, after):
    def body(array_ref, after_ref, out):
        pass

    return pl.pallas_call(
        body,
        out_shape=jax.ShapeDtypeStruct(array.shape, array.dtype),
        in_specs=[VMEM, ANY],
        out_specs=VMEM,
        input_output_aliases={0: 0},
        compiler_params=pltpu.CompilerParams(vmem_limit_bytes=12 * MIB),
    )(array, after)


def part(which, size):
    return pl.ds(pl.multiple_of(which * size, size), size)


def add(one, two, dtype):
    return (one.astype(F32) + two.astype(F32)).astype(dtype)


def columns_of(refs, rows):
    at = 0
    for ref in refs:
        yield at, ref[rows, :]
        at += ref.shape[1]


def pick(scalars, bit, arrays, after=None):
    size = arrays[0].shape[0] // 2
    width = pl.cdiv(sum(a.shape[1] for a in arrays), 128) * 128

    def body(scalars, *refs):
        for at, values in columns_of(refs[:-1], part(1 - scalars[bit], size)):
            refs[-1][:, pl.ds(at, values.shape[1])] = values

    return run(scalars, body, [((size, width), arrays[0].dtype)], arrays, after)[0]


def add_split(scalars, before, bit, arrays, got, after=None):
    def body(scalars, *refs):
        which = scalars[bit]
        size = got.shape[0] // 2
        for out, side in ((refs[-2], which), (refs[-1], 1 - which)):
            start = pl.multiple_of((2 * scalars[before] + side) * size, size)
            for at, values in columns_of(refs[: len(arrays)], pl.ds(start, size)):
                columns = pl.ds(at, values.shape[1])
                out[:, columns] = add(values, refs[len(arrays)][part(side, size), columns], out.dtype)

    return run(scalars, body, [((got.shape[0] // 2, got.shape[1]), got.dtype)] * 2, [*arrays, got], after)


def join(scalars, bit, pairs, after=None):
    rows = sum(2 * own.shape[0] for own, _ in pairs)

    def body(scalars, *refs):
        which, at = scalars[bit], 0
        for i, (own, _) in enumerate(pairs):
            size = own.shape[0]
            for place, ref in ((which, refs[2 * i]), (1 - which, refs[2 * i + 1])):
                refs[-1][pl.ds(pl.multiple_of(at + place * size, 16), size), :] = ref[...]
            at += 2 * size

    own = pairs[0][0]
    return run(scalars, body, [((rows, own.shape[1]), own.dtype)], [a for pair in pairs for a in pair], after)[0]


def join_chips(scalars, own, got):
    size = own.shape[0] // 2

    def body(scalars, own_ref, got_ref, out):
        for side, ref in ((scalars[CORE], own_ref), (1 - scalars[CORE], got_ref)):
            for chip in range(2):
                rows = pl.ds(pl.multiple_of((2 * chip + side) * size, size), size)
                out[rows, :] = ref[pl.ds(chip * size, size), :]

    return run(scalars, body, [((4 * size, own.shape[1]), own.dtype)], [own, got])[0]


def activate(scalars, kept, got, after=None):
    def body(scalars, kept_ref, got_ref, out):
        width = out.shape[1]
        gate, up = (
            kept_ref[:, pl.ds(at, width)].astype(F32) + got_ref[:, pl.ds(at, width)].astype(F32) for at in (0, width)
        )
        out[...] = (gate / (1.0 + jnp.exp(-gate)) * up).astype(BF16)

    return run(scalars, body, [((kept.shape[0], kept.shape[1] // 2), BF16)], [kept, got], after)[0]


def other_core(scalars, ffn):
    size = ffn.shape[0] // 8

    def body(scalars, ref, out):
        for chip in range(4):
            start = pl.multiple_of((2 * chip + 1 - scalars[CORE]) * size, size)
            out[pl.ds(chip * size, size), :] = ref[pl.ds(start, size), :]

    return run(scalars, body, [((4 * size, ffn.shape[1]), ffn.dtype)], [ffn])[0]


def add_cores(scalars, ffn, got):
    size = ffn.shape[0] // 8

    def body(scalars, ref, got_ref, stay, go):
        core = scalars[CORE]
        for out, chips in ((stay, (0, 2 - core)), (go, (1 + core, 3))):
            for i, chip in enumerate(chips):
                rows = pl.ds(pl.multiple_of((2 * chip + core) * size, size), size)
                out[pl.ds(i * size, size), :] = add(ref[rows, :], got_ref[part(chip, size), :], out.dtype)

    return run(scalars, body, [((2 * size, ffn.shape[1]), ffn.dtype)] * 2, [ffn, got])


def add_halves(scalars, stay, got):
    size = stay.shape[0] // 2

    def body(scalars, stay_ref, got_ref, first, second):
        for at, out in ((0, first), (size, second)):
            rows = pl.ds(at, size)
            out[...] = add(stay_ref[rows, :], got_ref[rows, :], out.dtype)

    return run(scalars, body, [((size, stay.shape[1]), stay.dtype)] * 2, [stay, got])


def residual(scalars, mine, at, kept, got):
    width = kept.shape[1]

    def body(scalars, mine_ref, kept_ref, got_ref, out):
        ffn = kept_ref[...].astype(F32) + got_ref[...].astype(F32)
        out[...] = (mine_ref[:, pl.ds(at, width)].astype(F32) + ffn).astype(BF16)

    return run(scalars, body, [(kept.shape, BF16)], [mine, kept, got])[0]


def stack(scalars, first, second, after=None):
    size = first.shape[0]

    def body(scalars, first_ref, second_ref, out, chosen):
        out[pl.ds(0, size), :] = first_ref[...]
        out[pl.ds(size, size), :] = second_ref[...]
        if after is not None:
            chosen[...] = jnp.where(scalars[CORE] == 0, first_ref[...], second_ref[...])

    outs = [((2 * size, first.shape[1]), first.dtype), (first.shape if after is not None else (16, 128), first.dtype)]
    return run(scalars, body, outs, [first, second], after)


def by_chip(scalars, pair, got):
    size = pair.shape[0] // 2

    def body(scalars, pair_ref, got_ref, out):
        core = scalars[CORE]
        for ref, chips in ((pair_ref, (0, 2 - core)), (got_ref, (1 + core, 3))):
            for i, chip in enumerate(chips):
                out[part(chip, size), :] = ref[pl.ds(i * size, size), :]

    return run(scalars, body, [((4 * size, pair.shape[1]), pair.dtype)], [pair, got])[0]


def scaled(scalars, owns, gots, gain):
    size, width = owns[0].shape[0] // 4, owns[0].shape[1]

    def body(scalars, *refs):
        own_refs, got_refs, (gain_ref, out, squares) = refs[: len(owns)], refs[len(owns) : 2 * len(owns)], refs[-3:]
        for side, side_refs in ((scalars[CORE], own_refs), (1 - scalars[CORE], got_refs)):
            for at in range(0, 4 * size, 16):
                start = (2 * (at // size) + side) * size + at % size
                rows = pl.ds(pl.multiple_of(start, 16), 16)
                total = 0.0
                for i, ref in enumerate(side_refs):
                    wide = ref[pl.ds(at, 16), :].astype(F32)
                    columns = pl.ds(i * width, width)
                    out[rows, columns] = (wide * gain_ref[:, columns]).astype(BF16)
                    total += jnp.sum(wide * wide, axis=1, keepdims=True)
                squares[rows, :] = jnp.broadcast_to(total, (16, 128))

    outs = [((8 * size, width * len(owns)), BF16), ((8 * size, 128), F32)]
    return run(scalars, body, outs, [*owns, *gots, gain])


def row_stats(scalars, kepts, gots, squares, more_squares, gold, columns):
    many, rows = len(kepts), kepts[0].shape[0]

    def body(scalars, *refs):
        squares_ref, more_ref, gold_ref, out, turn = refs[2 * many :]
        for at in range(0, rows, 16):
            block = pl.ds(at, 16)
            scale = lax.rsqrt((squares_ref[block, :1] + more_ref[block, :1]) / D + 1e-05)
            first, chunks = 0, []
            for kept, got in zip(refs[:many], refs[many : 2 * many]):
                logits = (kept[block, :].astype(F32) + got[block, :].astype(F32)) * scale
                column = lax.broadcasted_iota(jnp.int32, logits.shape, 1) + first
                chunks.append((jnp.where(column < columns, logits, -jnp.inf), column))
                first += logits.shape[1]
            top = functools.reduce(jnp.maximum, [jnp.max(c, axis=1, keepdims=True) for c, _ in chunks])
            total, picked = 0.0, 0.0
            for logits, column in chunks:
                total += jnp.sum(jnp.exp(logits - top), axis=1, keepdims=True)
                hit = (column + scalars[OFFSET] == gold_ref[block, :]) & (column < columns)
                picked += jnp.sum(jnp.where(hit, logits, 0.0), axis=1, keepdims=True)
            lane = lax.broadcasted_iota(jnp.int32, (16, 128), 1)
            turn[block, :] = jnp.where(lane == 0, top, jnp.where(lane == 1, total, picked))
        out[...] = turn[...].T[:8]

    return pl.pallas_call(
        body,
        out_shape=jax.ShapeDtypeStruct((8, rows), F32),
        in_specs=[SMEM, *[VMEM] * (2 * many + 3)],
        out_specs=VMEM,
        scratch_shapes=[pltpu.VMEM((rows, 128), F32)],
        compiler_params=pltpu.CompilerParams(vmem_limit_bytes=12 * MIB),
    )(scalars, *kepts, *gots, squares, more_squares, gold)


def swapper(n_dm, n_hv, on_dm, flip_of):
    pairs = []
    for dm in range(n_dm):
        for hv in range(n_hv):
            flip = flip_of(hv)
            to = (dm ^ flip, hv) if on_dm else (dm, hv ^ flip)
            pairs.append((dm * n_hv + hv, to[0] * n_hv + to[1]))
    return lambda array: lax.ppermute(array, ("dm", "hv"), pairs)


def on_blocks(
    tokens, gate_weight, up_weight, down_weight, norm_gain, unembed, gold_ids, option_lengths, *, n_dm, n_hv
):
    dm, hv = lax.axis_index("dm"), lax.axis_index("hv")
    core, chip = hv & 1, hv >> 1
    dm_first, dm_last = (dm >> core) & 1, (dm >> (1 - core)) & 1
    scalars = jnp.stack([dm_first, dm_last, core, hv * unembed.shape[1]]).astype(jnp.int32)
    z_first, z_last = (swapper(n_dm, n_hv, True, flip) for flip in (lambda hv: 1 << (hv & 1), lambda hv: 2 >> (hv & 1)))
    cores, x, y, xy_first, xy_last = (
        swapper(n_dm, n_hv, False, flip)
        for flip in (lambda hv: 1, lambda hv: 2, lambda hv: 4, lambda hv: 2 << (hv & 1), lambda hv: 4 >> (hv & 1))
    )
    gain = norm_gain[None, :]
    chip_rows = 2 * tokens.shape[0]

    def sums(piece):
        both = [jnp.dot(piece, weight, preferred_element_type=F32).astype(BF16) for weight in (gate_weight, up_weight)]
        return both, pick(scalars, DM_FIRST, both)

    from_core, from_x, from_y = cores(tokens), x(tokens), y(tokens)
    both_0, sent_0 = sums(join(scalars, CORE, [(tokens, from_core)]))
    got_0 = z_first(sent_0)
    beside, chosen = stack(scalars, from_x, from_y, sent_0)
    across = xy_last(chosen)
    both_1, sent_1 = sums(join_chips(scalars, beside, cores(beside)))
    got_1 = z_first(sent_1)
    kept_0, sent_0 = add_split(scalars, DM_FIRST, DM_LAST, both_0, got_0, sent_1)
    got_0 = z_last(sent_0)
    both_2, sent_2 = sums(join(scalars, CORE, [(across, cores(across))], kept_0))
    got_2 = z_first(sent_2)
    own_0 = activate(scalars, kept_0, got_0, sent_2)
    got_0 = z_last(own_0)
    kept_1, sent_1 = add_split(scalars, DM_FIRST, DM_LAST, both_1, got_1, own_0)
    got_1 = z_last(sent_1)
    own_0 = join(scalars, DM_LAST, [(own_0, got_0)], kept_1)
    got_0 = z_first(own_0)
    kept_2, sent_2 = add_split(scalars, DM_FIRST, DM_LAST, both_2, got_2, own_0)
    got_2 = z_last(sent_2)
    own_1 = activate(scalars, kept_1, got_1, kept_2)
    got_1 = z_last(own_1)
    own_2 = activate(scalars, kept_2, got_2, own_1)
    got_2 = z_last(own_2)
    own_1 = join(scalars, DM_LAST, [(own_1, got_1)], own_2)
    got_1 = z_first(own_1)
    own_2 = join(scalars, DM_LAST, [(own_2, got_2)], own_1)
    hidden = join(scalars, DM_FIRST, [(own_0, got_0), (own_1, got_1), (own_2, z_first(own_2))])
    owns, gots = [], []
    width = down_weight.shape[1] // DOWN_CHUNKS
    for at in range(0, down_weight.shape[1], width):
        ffn = jnp.dot(hidden, down_weight[:, at : at + width], preferred_element_type=F32).astype(BF16)
        stay, go = add_cores(scalars, ffn, cores(other_core(scalars, ffn)))
        stay, go = add_halves(scalars, stay, xy_first(go))
        resid = residual(scalars, tokens, at, stay, xy_last(go))
        pair, _ = stack(scalars, resid, xy_last(resid))
        owns.append(by_chip(scalars, pair, xy_first(pair)))
        gots.append(cores(owns[-1]))
    left, squares = scaled(scalars, owns, gots, gain)
    sent_squares = pick(scalars, DM_FIRST, [squares])
    got_squares = z_first(sent_squares)
    left = tie(left, sent_squares)
    kepts, gots, first = [], [], None
    for at in range(0, unembed.shape[1], VOCAB_TILE):
        logits = jnp.dot(left, unembed[:, at : at + VOCAB_TILE], preferred_element_type=F32).astype(BF16)
        sent = pick(scalars, DM_FIRST, [logits])
        got = z_first(sent)
        if first is None:
            last, sent_squares = add_split(scalars, DM_FIRST, DM_LAST, [squares], got_squares, sent)
            kept_squares, got_squares = last, z_last(sent_squares)
        else:
            last, sent = add_split(scalars, DM_FIRST, DM_LAST, *first, sent)
            kepts.append(last)
            gots.append(z_last(sent))
        first = ([logits], got)
        if at + VOCAB_TILE < unembed.shape[1]:
            left = tie(left, last)
    last, sent = add_split(scalars, DM_FIRST, DM_LAST, *first, last)
    kepts.append(last)
    gots.append(z_last(sent))
    gold = lax.dynamic_slice_in_dim(gold_ids, (chip ^ (2 * dm_first + dm_last)) * chip_rows, chip_rows)
    stats = row_stats(scalars, kepts, gots, kept_squares, got_squares, gold[:, None], unembed.shape[1])
    stats = stats[None]
    for bit, swap in ((dm_last, z_last), (dm_first, z_first)):
        got = swap(stats)
        stats = jnp.concatenate([jnp.where(bit == 0, stats, got), jnp.where(bit == 0, got, stats)])
    stats = stats.reshape(2, 2, 8, chip_rows)
    stats = jnp.where(chip & 1 == 0, stats, stats[:, ::-1])
    stats = jnp.where(chip >> 1 == 0, stats, stats[::-1])
    stats = lax.all_gather(stats.reshape(4, 8, chip_rows), "hv", axis=0)
    top = jnp.max(stats[:, :, 0], axis=0)
    total = jnp.sum(stats[:, :, 1] * jnp.exp(stats[:, :, 0] - top), axis=0)
    return (jnp.sum(stats[:, :, 2], axis=0) - top - jnp.log(total)).reshape(-1)


def on_any_mesh(
    tokens, gate_weight, up_weight, down_weight, norm_gain, unembed, gold_ids, option_lengths, *, n_dm, n_hv
):
    piece = lax.all_gather(tokens, "hv", axis=0, tiled=True)
    gate, up = (
        lax.psum_scatter(
            jnp.dot(piece, weight, preferred_element_type=F32), "dm", scatter_dimension=0, tiled=True
        )
        for weight in (gate_weight, up_weight)
    )
    hidden = lax.all_gather((jax.nn.silu(gate) * up).astype(BF16), "dm", axis=0, tiled=True)
    ffn = jnp.dot(hidden, down_weight, preferred_element_type=F32)
    ffn = lax.psum_scatter(ffn, "hv", scatter_dimension=0, tiled=True)
    resid = (tokens.astype(F32) + ffn).astype(BF16)
    wide = resid.astype(F32)
    squares = lax.psum(jnp.sum(wide * wide, axis=1), "dm")
    normed = (wide * lax.rsqrt(squares[:, None] / D + 1e-05) * norm_gain).astype(BF16)
    normed = lax.all_gather(normed, "hv", axis=0, tiled=True)
    logits = jnp.dot(normed, unembed, preferred_element_type=F32)
    logits = lax.psum_scatter(logits, "dm", scatter_dimension=0, tiled=True)
    rows = logits.shape[0]
    gold = lax.dynamic_slice_in_dim(gold_ids, lax.axis_index("dm") * rows, rows)
    hit = lax.broadcasted_iota(jnp.int32, logits.shape, 1) + lax.axis_index("hv") * unembed.shape[1] == gold[:, None]
    top = lax.pmax(jnp.max(logits, axis=1), "hv")
    total, gold = lax.psum(
        (jnp.sum(jnp.exp(logits - top[:, None]), axis=1), jnp.sum(jnp.where(hit, logits, 0.0), axis=1)), "hv"
    )
    return lax.all_gather(gold - top - jnp.log(total), "dm", axis=0, tiled=True)


def per_device(*args, n_dm, n_hv):
    rows = on_blocks if (n_dm, n_hv) == (4, 8) else on_any_mesh
    token_logprob = rows(*args, n_dm=n_dm, n_hv=n_hv)
    option_lengths = args[-1]
    ends = jnp.cumsum(option_lengths)
    starts = ends - option_lengths
    places = jnp.arange(token_logprob.shape[0], dtype=jnp.int32)
    member = ((places[None, :] >= starts[:, None]) & (places[None, :] < ends[:, None])).astype(F32)
    option_sums = jnp.dot(member, token_logprob, precision=lax.Precision.HIGHEST)
    option_score = option_sums / option_lengths.astype(F32)
    return (token_logprob, option_score)


def solution(mesh):
    placed = (
        P("hv", "dm"),
        P("dm", "hv"),
        P("dm", "hv"),
        P("hv", "dm"),
        P("dm"),
        P("dm", "hv"),
        P(),
        P(),
    )
    body = functools.partial(per_device, n_dm=mesh.shape["dm"], n_hv=mesh.shape["hv"])
    return jax.shard_map(
        body, mesh=mesh, in_specs=placed, out_specs=(P(), P()), check_vma=False
    )
```

```python
import functools

import jax
import jax.numpy as jnp
from jax import lax
from jax.experimental import pallas as pl
from jax.experimental.pallas import tpu as pltpu
from jax.sharding import PartitionSpec as P

D = 16384
DOWN_CHUNKS = 2
VOCAB_TILE = 1024
F32 = jnp.float32
BF16 = jnp.bfloat16
MIB = 1 << 20
VMEM = pl.BlockSpec(memory_space=pltpu.VMEM)
SMEM = pl.BlockSpec(memory_space=pltpu.SMEM)
ANY = pl.BlockSpec(memory_space=pl.ANY)
DM_FIRST, DM_LAST, CORE, OFFSET = range(4)


def run(scalars, body, outs, arrays, after=None):
    ahead = [] if after is None else [after]

    def kernel(scalars, *refs):
        body(scalars, *refs[: len(arrays)], *refs[len(arrays) + len(ahead) :])

    return pl.pallas_call(
        kernel,
        out_shape=[jax.ShapeDtypeStruct(*out) for out in outs],
        in_specs=[SMEM, *[VMEM] * len(arrays), *[ANY] * len(ahead)],
        out_specs=[VMEM] * len(outs),
        compiler_params=pltpu.CompilerParams(vmem_limit_bytes=12 * MIB),
        cost_estimate=pl.CostEstimate(
            flops=0, bytes_accessed=2 * sum(a.size * a.dtype.itemsize for a in arrays), transcendentals=0
        ),
    )(scalars, *arrays, *ahead)


def tie(array, after):
    def body(array_ref, after_ref, out):
        pass

    return pl.pallas_call(
        body,
        out_shape=jax.ShapeDtypeStruct(array.shape, array.dtype),
        in_specs=[VMEM, ANY],
        out_specs=VMEM,
        input_output_aliases={0: 0},
        compiler_params=pltpu.CompilerParams(vmem_limit_bytes=12 * MIB),
    )(array, after)


def part(which, size):
    return pl.ds(pl.multiple_of(which * size, size), size)


def add(one, two, dtype):
    return (one.astype(F32) + two.astype(F32)).astype(dtype)


def columns_of(refs, rows):
    at = 0
    for ref in refs:
        yield at, ref[rows, :]
        at += ref.shape[1]


def pick(scalars, bit, arrays, after=None):
    size = arrays[0].shape[0] // 2
    width = pl.cdiv(sum(a.shape[1] for a in arrays), 128) * 128

    def body(scalars, *refs):
        for at, values in columns_of(refs[:-1], part(1 - scalars[bit], size)):
            refs[-1][:, pl.ds(at, values.shape[1])] = values

    return run(scalars, body, [((size, width), arrays[0].dtype)], arrays, after)[0]


def add_split(scalars, before, bit, arrays, got, after=None):
    def body(scalars, *refs):
        which = scalars[bit]
        size = got.shape[0] // 2
        for out, side in ((refs[-2], which), (refs[-1], 1 - which)):
            start = pl.multiple_of((2 * scalars[before] + side) * size, size)
            for at, values in columns_of(refs[: len(arrays)], pl.ds(start, size)):
                columns = pl.ds(at, values.shape[1])
                out[:, columns] = add(values, refs[len(arrays)][part(side, size), columns], out.dtype)

    return run(scalars, body, [((got.shape[0] // 2, got.shape[1]), got.dtype)] * 2, [*arrays, got], after)


def add_half(scalars, before, arrays, got, after=None):
    def body(scalars, *refs):
        size = got.shape[0]
        for at, values in columns_of(refs[: len(arrays)], part(scalars[before], size)):
            columns = pl.ds(at, values.shape[1])
            refs[-1][:, columns] = add(values, refs[len(arrays)][:, columns], got.dtype)

    return run(scalars, body, [(got.shape, got.dtype)], [*arrays, got], after)[0]


def join(scalars, bit, pairs, after=None):
    rows = sum(2 * own.shape[0] for own, _ in pairs)

    def body(scalars, *refs):
        which, at = scalars[bit], 0
        for i, (own, _) in enumerate(pairs):
            size = own.shape[0]
            for place, ref in ((which, refs[2 * i]), (1 - which, refs[2 * i + 1])):
                refs[-1][pl.ds(pl.multiple_of(at + place * size, 16), size), :] = ref[...]
            at += 2 * size

    own = pairs[0][0]
    return run(scalars, body, [((rows, own.shape[1]), own.dtype)], [a for pair in pairs for a in pair], after)[0]


def join_below(scalars, above, pairs):
    rows = above.shape[0] + sum(2 * own.shape[0] for own, _ in pairs)

    def body(scalars, above_ref, *refs):
        refs[-1][pl.ds(0, above.shape[0]), :] = above_ref[...]
        which, at = scalars[DM_FIRST], above.shape[0]
        for i, (own, _) in enumerate(pairs):
            size = own.shape[0]
            for place, ref in ((which, refs[2 * i]), (1 - which, refs[2 * i + 1])):
                refs[-1][pl.ds(pl.multiple_of(at + place * size, 16), size), :] = ref[...]
            at += 2 * size

    arrays = [above, *[array for pair in pairs for array in pair]]
    return run(scalars, body, [((rows, above.shape[1]), above.dtype)], arrays)[0]


def join_chips(scalars, own, got):
    size = own.shape[0] // 2

    def body(scalars, own_ref, got_ref, out):
        for side, ref in ((scalars[CORE], own_ref), (1 - scalars[CORE], got_ref)):
            for chip in range(2):
                rows = pl.ds(pl.multiple_of((2 * chip + side) * size, size), size)
                out[rows, :] = ref[pl.ds(chip * size, size), :]

    return run(scalars, body, [((4 * size, own.shape[1]), own.dtype)], [own, got])[0]


def activate(scalars, kept, got, after=None):
    def body(scalars, kept_ref, got_ref, out):
        width = out.shape[1]
        gate, up = (
            kept_ref[:, pl.ds(at, width)].astype(F32) + got_ref[:, pl.ds(at, width)].astype(F32) for at in (0, width)
        )
        out[...] = (gate / (1.0 + jnp.exp(-gate)) * up).astype(BF16)

    return run(scalars, body, [((kept.shape[0], kept.shape[1] // 2), BF16)], [kept, got], after)[0]


def other_core(scalars, ffn):
    size = ffn.shape[0] // 8

    def body(scalars, ref, out):
        for chip in range(4):
            start = pl.multiple_of((2 * chip + 1 - scalars[CORE]) * size, size)
            out[pl.ds(chip * size, size), :] = ref[pl.ds(start, size), :]

    return run(scalars, body, [((4 * size, ffn.shape[1]), ffn.dtype)], [ffn])[0]


def add_cores(scalars, ffn, got):
    size = ffn.shape[0] // 8

    def body(scalars, ref, got_ref, stay, go):
        core = scalars[CORE]
        for out, chips in ((stay, (0, 2 - core)), (go, (1 + core, 3))):
            for i, chip in enumerate(chips):
                rows = pl.ds(pl.multiple_of((2 * chip + core) * size, size), size)
                out[pl.ds(i * size, size), :] = add(ref[rows, :], got_ref[part(chip, size), :], out.dtype)

    return run(scalars, body, [((2 * size, ffn.shape[1]), ffn.dtype)] * 2, [ffn, got])


def add_halves(scalars, stay, got):
    size = stay.shape[0] // 2

    def body(scalars, stay_ref, got_ref, first, second):
        for at, out in ((0, first), (size, second)):
            rows = pl.ds(at, size)
            out[...] = add(stay_ref[rows, :], got_ref[rows, :], out.dtype)

    return run(scalars, body, [((size, stay.shape[1]), stay.dtype)] * 2, [stay, got])


def residual(scalars, mine, at, kept, got):
    width = kept.shape[1]

    def body(scalars, mine_ref, kept_ref, got_ref, out):
        ffn = kept_ref[...].astype(F32) + got_ref[...].astype(F32)
        out[...] = (mine_ref[:, pl.ds(at, width)].astype(F32) + ffn).astype(BF16)

    return run(scalars, body, [(kept.shape, BF16)], [mine, kept, got])[0]


def stack(scalars, first, second, after=None):
    size = first.shape[0]

    def body(scalars, first_ref, second_ref, out, chosen):
        out[pl.ds(0, size), :] = first_ref[...]
        out[pl.ds(size, size), :] = second_ref[...]
        if after is not None:
            chosen[...] = jnp.where(scalars[CORE] == 0, first_ref[...], second_ref[...])

    outs = [((2 * size, first.shape[1]), first.dtype), (first.shape if after is not None else (16, 128), first.dtype)]
    return run(scalars, body, outs, [first, second], after)


def moved(scalars, array, after):
    def body(scalars, ref, out):
        out[...] = ref[...]

    return run(scalars, body, [(array.shape, array.dtype)], [array], after)[0]


def by_chip(scalars, pair, got):
    size = pair.shape[0] // 2

    def body(scalars, pair_ref, got_ref, out):
        core = scalars[CORE]
        for ref, chips in ((pair_ref, (0, 2 - core)), (got_ref, (1 + core, 3))):
            for i, chip in enumerate(chips):
                out[part(chip, size), :] = ref[pl.ds(i * size, size), :]

    return run(scalars, body, [((4 * size, pair.shape[1]), pair.dtype)], [pair, got])[0]


def scaled(scalars, owns, gots, gain):
    size, width = owns[0].shape[0] // 4, owns[0].shape[1]

    def body(scalars, *refs):
        own_refs, got_refs, (gain_ref, out, squares) = refs[: len(owns)], refs[len(owns) : 2 * len(owns)], refs[-3:]
        for side, side_refs in ((scalars[CORE], own_refs), (1 - scalars[CORE], got_refs)):
            for at in range(0, 4 * size, 16):
                start = (2 * (at // size) + side) * size + at % size
                rows = pl.ds(pl.multiple_of(start, 16), 16)
                total = 0.0
                for i, ref in enumerate(side_refs):
                    wide = ref[pl.ds(at, 16), :].astype(F32)
                    columns = pl.ds(i * width, width)
                    out[rows, columns] = (wide * gain_ref[:, columns]).astype(BF16)
                    total += jnp.sum(wide * wide, axis=1, keepdims=True)
                squares[rows, :] = jnp.broadcast_to(total, (16, 128))

    outs = [((8 * size, width * len(owns)), BF16), ((8 * size, 128), F32)]
    return run(scalars, body, outs, [*owns, *gots, gain])


def row_scale(scalars, squares, more_squares, after):
    def body(scalars, squares_ref, more_ref, out):
        out[...] = lax.rsqrt((squares_ref[...] + more_ref[...]) / D + 1e-05)

    return run(scalars, body, [(squares.shape, F32)], [squares, more_squares], after)[0]


def row_stats(scalars, kepts, gots, scale, gold, first, columns, before=None, after=None):
    many, rows = len(kepts), kepts[0].shape[0]
    others = [] if before is None else [before]

    def body(scalars, *refs):
        scale_ref, gold_ref, *before_refs, out = refs[2 * many :]
        blocks = []
        for at in range(0, rows, 16):
            block = pl.ds(at, 16)
            start, chunks = first, []
            for kept, got in zip(refs[:many], refs[many : 2 * many]):
                logits = (kept[block, :].astype(F32) + got[block, :].astype(F32)) * scale_ref[block, :1]
                column = lax.broadcasted_iota(jnp.int32, logits.shape, 1) + start
                chunks.append((jnp.where(column < columns, logits, -jnp.inf), column))
                start += logits.shape[1]
            tops = [jnp.max(logits, axis=1, keepdims=True) for logits, _ in chunks]
            tops += [ref[block, 0:1] for ref in before_refs]
            top = functools.reduce(jnp.maximum, tops)
            total, picked = 0.0, 0.0
            for logits, column in chunks:
                total += jnp.sum(jnp.exp(logits - top), axis=1, keepdims=True)
                hit = (column + scalars[OFFSET] == gold_ref[block, :]) & (column < columns)
                picked += jnp.sum(jnp.where(hit, logits, 0.0), axis=1, keepdims=True)
            for ref in before_refs:
                total += ref[block, 1:2] * jnp.exp(ref[block, 0:1] - top)
                picked += ref[block, 2:3]
            lane = lax.broadcasted_iota(jnp.int32, (16, 128), 1)
            blocks.append(jnp.where(lane == 0, top, jnp.where(lane == 1, total, picked)))
        blocks = jnp.concatenate(blocks)
        out[...] = blocks if before is None else blocks.T[:8]

    outs = [((rows, 128) if before is None else (8, rows), F32)]
    return run(scalars, body, outs, [*kepts, *gots, scale, gold, *others], after)[0]


def swapper(n_dm, n_hv, on_dm, flip_of):
    pairs = []
    for dm in range(n_dm):
        for hv in range(n_hv):
            flip = flip_of(hv)
            to = (dm ^ flip, hv) if on_dm else (dm, hv ^ flip)
            pairs.append((dm * n_hv + hv, to[0] * n_hv + to[1]))
    return lambda array: lax.ppermute(array, ("dm", "hv"), pairs)


def on_blocks(
    tokens, gate_weight, up_weight, down_weight, norm_gain, unembed, gold_ids, option_lengths, *, n_dm, n_hv
):
    dm, hv = lax.axis_index("dm"), lax.axis_index("hv")
    core, chip = hv & 1, hv >> 1
    dm_first, dm_last = (dm >> core) & 1, (dm >> (1 - core)) & 1
    scalars = jnp.stack([dm_first, dm_last, core, hv * unembed.shape[1]]).astype(jnp.int32)
    z_first, z_last = (swapper(n_dm, n_hv, True, flip) for flip in (lambda hv: 1 << (hv & 1), lambda hv: 2 >> (hv & 1)))
    cores, x, y, xy_first, xy_last = (
        swapper(n_dm, n_hv, False, flip)
        for flip in (lambda hv: 1, lambda hv: 2, lambda hv: 4, lambda hv: 2 << (hv & 1), lambda hv: 4 >> (hv & 1))
    )
    gain = norm_gain[None, :]
    chip_rows = 2 * tokens.shape[0]

    def sums(piece):
        both = [jnp.dot(piece, weight, preferred_element_type=F32).astype(BF16) for weight in (gate_weight, up_weight)]
        return both, pick(scalars, DM_FIRST, both)

    tokens = jnp.where(dm < n_dm, tokens, 0)
    from_core, from_x, from_y = cores(tokens), x(tokens), y(tokens)
    both_0, sent_0 = sums(join(scalars, CORE, [(tokens, from_core)]))
    got_0 = z_first(sent_0)
    beside, chosen = stack(scalars, from_x, from_y, sent_0)
    across = xy_last(chosen)
    both_1, sent_1 = sums(join_chips(scalars, beside, cores(beside)))
    got_1 = z_first(sent_1)
    half_0 = add_half(scalars, DM_FIRST, both_0, got_0, sent_1)
    got_0 = z_last(half_0)
    across = moved(scalars, across, half_0)
    both_2, sent_2 = sums(join(scalars, CORE, [(across, cores(across))]))
    got_2 = z_first(sent_2)
    own_0 = activate(scalars, half_0, got_0, sent_2)
    got_0 = z_first(own_0)
    kept_1, sent_1 = add_split(scalars, DM_FIRST, DM_LAST, both_1, got_1, own_0)
    got_1 = z_last(sent_1)
    half_2 = add_half(scalars, DM_FIRST, both_2, got_2, kept_1)
    got_2 = z_last(half_2)
    own_1 = activate(scalars, kept_1, got_1, half_2)
    got_1 = z_last(own_1)
    whole_0 = join(scalars, DM_FIRST, [(own_0, got_0)], own_1)
    own_2 = activate(scalars, half_2, got_2, whole_0)
    got_2 = z_first(own_2)
    own_1 = join(scalars, DM_LAST, [(own_1, got_1)], own_2)
    hidden = join_below(scalars, whole_0, [(own_1, z_first(own_1)), (own_2, got_2)])
    owns, gots = [], []
    width = down_weight.shape[1] // DOWN_CHUNKS
    for at in range(0, down_weight.shape[1], width):
        ffn = jnp.dot(hidden, down_weight[:, at : at + width], preferred_element_type=F32).astype(BF16)
        stay, go = add_cores(scalars, ffn, cores(other_core(scalars, ffn)))
        stay, go = add_halves(scalars, stay, xy_first(go))
        resid = residual(scalars, tokens, at, stay, xy_last(go))
        pair, _ = stack(scalars, resid, xy_last(resid))
        owns.append(by_chip(scalars, pair, xy_first(pair)))
        gots.append(cores(owns[-1]))
    left, squares = scaled(scalars, owns, gots, gain)
    gold = lax.dynamic_slice_in_dim(gold_ids, (chip ^ (2 * dm_first + dm_last)) * chip_rows, chip_rows)[:, None]
    sent_squares = pick(scalars, DM_FIRST, [squares])
    got_squares = z_first(sent_squares)
    left = tie(left, sent_squares)
    kepts, gots, first, scale = [], [], None, None
    for at in range(0, unembed.shape[1], VOCAB_TILE):
        logits = jnp.dot(left, unembed[:, at : at + VOCAB_TILE], preferred_element_type=F32).astype(BF16)
        sent = pick(scalars, DM_FIRST, [logits])
        got = z_first(sent)
        if first is None:
            last, sent_squares = add_split(scalars, DM_FIRST, DM_LAST, [squares], got_squares, sent)
            kept_squares, got_squares = last, z_last(sent_squares)
        else:
            if scale is None:
                sent = scale = row_scale(scalars, kept_squares, got_squares, sent)
            last, sent = add_split(scalars, DM_FIRST, DM_LAST, *first, sent)
            kepts.append(last)
            gots.append(z_last(sent))
        first = ([logits], got)
        if at + VOCAB_TILE < unembed.shape[1]:
            left = tie(left, last)
    last, sent = add_split(scalars, DM_FIRST, DM_LAST, *first, last)
    columns = unembed.shape[1]
    stats = row_stats(scalars, kepts, gots, scale, gold, 0, columns, None, last)
    stats = row_stats(scalars, [last], [z_last(sent)], scale, gold, VOCAB_TILE * len(kepts), columns, stats)
    stats = stats[None]
    for bit, swap in ((dm_last, z_last), (dm_first, z_first)):
        got = swap(stats)
        stats = jnp.concatenate([jnp.where(bit == 0, stats, got), jnp.where(bit == 0, got, stats)])
    stats = stats.reshape(2, 2, 8, chip_rows)
    stats = jnp.where(chip & 1 == 0, stats, stats[:, ::-1])
    stats = jnp.where(chip >> 1 == 0, stats, stats[::-1])
    stats = lax.all_gather(stats.reshape(4, 8, chip_rows), "hv", axis=0)
    top = jnp.max(stats[:, :, 0], axis=0)
    total = jnp.sum(stats[:, :, 1] * jnp.exp(stats[:, :, 0] - top), axis=0)
    return (jnp.sum(stats[:, :, 2], axis=0) - top - jnp.log(total)).reshape(-1)


def on_any_mesh(
    tokens, gate_weight, up_weight, down_weight, norm_gain, unembed, gold_ids, option_lengths, *, n_dm, n_hv
):
    piece = lax.all_gather(tokens, "hv", axis=0, tiled=True)
    gate, up = (
        lax.psum_scatter(
            jnp.dot(piece, weight, preferred_element_type=F32), "dm", scatter_dimension=0, tiled=True
        )
        for weight in (gate_weight, up_weight)
    )
    hidden = lax.all_gather((jax.nn.silu(gate) * up).astype(BF16), "dm", axis=0, tiled=True)
    ffn = jnp.dot(hidden, down_weight, preferred_element_type=F32)
    ffn = lax.psum_scatter(ffn, "hv", scatter_dimension=0, tiled=True)
    resid = (tokens.astype(F32) + ffn).astype(BF16)
    wide = resid.astype(F32)
    squares = lax.psum(jnp.sum(wide * wide, axis=1), "dm")
    normed = (wide * lax.rsqrt(squares[:, None] / D + 1e-05) * norm_gain).astype(BF16)
    normed = lax.all_gather(normed, "hv", axis=0, tiled=True)
    logits = jnp.dot(normed, unembed, preferred_element_type=F32)
    logits = lax.psum_scatter(logits, "dm", scatter_dimension=0, tiled=True)
    rows = logits.shape[0]
    gold = lax.dynamic_slice_in_dim(gold_ids, lax.axis_index("dm") * rows, rows)
    hit = lax.broadcasted_iota(jnp.int32, logits.shape, 1) + lax.axis_index("hv") * unembed.shape[1] == gold[:, None]
    top = lax.pmax(jnp.max(logits, axis=1), "hv")
    total, gold = lax.psum(
        (jnp.sum(jnp.exp(logits - top[:, None]), axis=1), jnp.sum(jnp.where(hit, logits, 0.0), axis=1)), "hv"
    )
    return lax.all_gather(gold - top - jnp.log(total), "dm", axis=0, tiled=True)


def per_device(*args, n_dm, n_hv):
    rows = on_blocks if (n_dm, n_hv) == (4, 8) else on_any_mesh
    token_logprob = rows(*args, n_dm=n_dm, n_hv=n_hv)
    option_lengths = args[-1]
    ends = jnp.cumsum(option_lengths)
    starts = ends - option_lengths
    places = jnp.arange(token_logprob.shape[0], dtype=jnp.int32)
    member = ((places[None, :] >= starts[:, None]) & (places[None, :] < ends[:, None])).astype(F32)
    option_sums = jnp.dot(member, token_logprob, precision=lax.Precision.HIGHEST)
    option_score = option_sums / option_lengths.astype(F32)
    return (token_logprob, option_score)


def solution(mesh):
    placed = (
        P("hv", "dm"),
        P("dm", "hv"),
        P("dm", "hv"),
        P("hv", "dm"),
        P("dm"),
        P("dm", "hv"),
        P(),
        P(),
    )
    body = functools.partial(per_device, n_dm=mesh.shape["dm"], n_hv=mesh.shape["hv"])
    return jax.shard_map(
        body, mesh=mesh, in_specs=placed, out_specs=(P(), P()), check_vma=False
    )
```

```python
import functools

import jax
import jax.numpy as jnp
from jax import lax
from jax.experimental import pallas as pl
from jax.experimental.pallas import tpu as pltpu
from jax.sharding import PartitionSpec as P

D = 16384
DOWN_CHUNKS = 2
VOCAB_TILE = 1024
F32 = jnp.float32
BF16 = jnp.bfloat16
MIB = 1 << 20
VMEM = pl.BlockSpec(memory_space=pltpu.VMEM)
SMEM = pl.BlockSpec(memory_space=pltpu.SMEM)
ANY = pl.BlockSpec(memory_space=pl.ANY)
DM_FIRST, DM_LAST, CORE, OFFSET = range(4)


def run(scalars, body, outs, arrays, after=None):
    ahead = [] if after is None else [after]

    def kernel(scalars, *refs):
        body(scalars, *refs[: len(arrays)], *refs[len(arrays) + len(ahead) :])

    return pl.pallas_call(
        kernel,
        out_shape=[jax.ShapeDtypeStruct(*out) for out in outs],
        in_specs=[SMEM, *[VMEM] * len(arrays), *[ANY] * len(ahead)],
        out_specs=[VMEM] * len(outs),
        compiler_params=pltpu.CompilerParams(vmem_limit_bytes=12 * MIB),
        cost_estimate=pl.CostEstimate(
            flops=0, bytes_accessed=2 * sum(a.size * a.dtype.itemsize for a in arrays), transcendentals=0
        ),
    )(scalars, *arrays, *ahead)


def tie(array, after):
    def body(array_ref, after_ref, out):
        pass

    return pl.pallas_call(
        body,
        out_shape=jax.ShapeDtypeStruct(array.shape, array.dtype),
        in_specs=[VMEM, ANY],
        out_specs=VMEM,
        input_output_aliases={0: 0},
        compiler_params=pltpu.CompilerParams(vmem_limit_bytes=12 * MIB),
    )(array, after)


def part(which, size):
    return pl.ds(pl.multiple_of(which * size, size), size)


def add(one, two, dtype):
    return (one.astype(F32) + two.astype(F32)).astype(dtype)


def columns_of(refs, rows):
    at = 0
    for ref in refs:
        yield at, ref[rows, :]
        at += ref.shape[1]


def pick(scalars, bit, arrays, after=None):
    size = arrays[0].shape[0] // 2
    width = pl.cdiv(sum(a.shape[1] for a in arrays), 128) * 128

    def body(scalars, *refs):
        for at, values in columns_of(refs[:-1], part(1 - scalars[bit], size)):
            refs[-1][:, pl.ds(at, values.shape[1])] = values

    return run(scalars, body, [((size, width), arrays[0].dtype)], arrays, after)[0]


def add_split(scalars, before, bit, arrays, got, after=None):
    def body(scalars, *refs):
        which = scalars[bit]
        size = got.shape[0] // 2
        for out, side in ((refs[-2], which), (refs[-1], 1 - which)):
            start = pl.multiple_of((2 * scalars[before] + side) * size, size)
            for at, values in columns_of(refs[: len(arrays)], pl.ds(start, size)):
                columns = pl.ds(at, values.shape[1])
                out[:, columns] = add(values, refs[len(arrays)][part(side, size), columns], out.dtype)

    return run(scalars, body, [((got.shape[0] // 2, got.shape[1]), got.dtype)] * 2, [*arrays, got], after)


def add_half(scalars, before, arrays, got, after=None):
    def body(scalars, *refs):
        size = got.shape[0]
        for at, values in columns_of(refs[: len(arrays)], part(scalars[before], size)):
            columns = pl.ds(at, values.shape[1])
            refs[-1][:, columns] = add(values, refs[len(arrays)][:, columns], got.dtype)

    return run(scalars, body, [(got.shape, got.dtype)], [*arrays, got], after)[0]


def join(scalars, bit, pairs, after=None):
    rows = sum(2 * own.shape[0] for own, _ in pairs)

    def body(scalars, *refs):
        which, at = scalars[bit], 0
        for i, (own, _) in enumerate(pairs):
            size = own.shape[0]
            for place, ref in ((which, refs[2 * i]), (1 - which, refs[2 * i + 1])):
                refs[-1][pl.ds(pl.multiple_of(at + place * size, 16), size), :] = ref[...]
            at += 2 * size

    own = pairs[0][0]
    return run(scalars, body, [((rows, own.shape[1]), own.dtype)], [a for pair in pairs for a in pair], after)[0]


def join_below(scalars, above, pairs):
    rows = above.shape[0] + sum(2 * own.shape[0] for _, own, _ in pairs)

    def body(scalars, above_ref, *refs):
        refs[-1][pl.ds(0, above.shape[0]), :] = above_ref[...]
        at = above.shape[0]
        for i, (bit, own, _) in enumerate(pairs):
            which, size = scalars[bit], own.shape[0]
            for place, ref in ((which, refs[2 * i]), (1 - which, refs[2 * i + 1])):
                refs[-1][pl.ds(pl.multiple_of(at + place * size, 16), size), :] = ref[...]
            at += 2 * size

    arrays = [above, *[array for _, *pair in pairs for array in pair]]
    return run(scalars, body, [((rows, above.shape[1]), above.dtype)], arrays)[0]


def join_chips(scalars, own, got):
    size = own.shape[0] // 2

    def body(scalars, own_ref, got_ref, out):
        for side, ref in ((scalars[CORE], own_ref), (1 - scalars[CORE], got_ref)):
            for chip in range(2):
                rows = pl.ds(pl.multiple_of((2 * chip + side) * size, size), size)
                out[rows, :] = ref[pl.ds(chip * size, size), :]

    return run(scalars, body, [((4 * size, own.shape[1]), own.dtype)], [own, got])[0]


def activate(scalars, kept, got, after=None):
    def body(scalars, kept_ref, got_ref, out):
        width = out.shape[1]
        gate, up = (
            kept_ref[:, pl.ds(at, width)].astype(F32) + got_ref[:, pl.ds(at, width)].astype(F32) for at in (0, width)
        )
        out[...] = (gate / (1.0 + jnp.exp(-gate)) * up).astype(BF16)

    return run(scalars, body, [((kept.shape[0], kept.shape[1] // 2), BF16)], [kept, got], after)[0]


def other_core(scalars, ffn):
    size = ffn.shape[0] // 8

    def body(scalars, ref, out):
        for chip in range(4):
            start = pl.multiple_of((2 * chip + 1 - scalars[CORE]) * size, size)
            out[pl.ds(chip * size, size), :] = ref[pl.ds(start, size), :]

    return run(scalars, body, [((4 * size, ffn.shape[1]), ffn.dtype)], [ffn])[0]


def add_cores(scalars, ffn, got):
    size = ffn.shape[0] // 8

    def body(scalars, ref, got_ref, stay, go):
        core = scalars[CORE]
        for out, chips in ((stay, (0, 2 - core)), (go, (1 + core, 3))):
            for i, chip in enumerate(chips):
                rows = pl.ds(pl.multiple_of((2 * chip + core) * size, size), size)
                out[pl.ds(i * size, size), :] = add(ref[rows, :], got_ref[part(chip, size), :], out.dtype)

    return run(scalars, body, [((2 * size, ffn.shape[1]), ffn.dtype)] * 2, [ffn, got])


def add_halves(scalars, stay, got):
    size = stay.shape[0] // 2

    def body(scalars, stay_ref, got_ref, first, second):
        for at, out in ((0, first), (size, second)):
            rows = pl.ds(at, size)
            out[...] = add(stay_ref[rows, :], got_ref[rows, :], out.dtype)

    return run(scalars, body, [((size, stay.shape[1]), stay.dtype)] * 2, [stay, got])


def residual(scalars, mine, at, kept, got):
    width = kept.shape[1]

    def body(scalars, mine_ref, kept_ref, got_ref, out):
        ffn = kept_ref[...].astype(F32) + got_ref[...].astype(F32)
        out[...] = (mine_ref[:, pl.ds(at, width)].astype(F32) + ffn).astype(BF16)

    return run(scalars, body, [(kept.shape, BF16)], [mine, kept, got])[0]


def stack(scalars, first, second, after=None):
    size = first.shape[0]

    def body(scalars, first_ref, second_ref, out, chosen):
        out[pl.ds(0, size), :] = first_ref[...]
        out[pl.ds(size, size), :] = second_ref[...]
        if after is not None:
            chosen[...] = jnp.where(scalars[CORE] == 0, first_ref[...], second_ref[...])

    outs = [((2 * size, first.shape[1]), first.dtype), (first.shape if after is not None else (16, 128), first.dtype)]
    return run(scalars, body, outs, [first, second], after)


def moved(scalars, array, after):
    def body(scalars, ref, out):
        out[...] = ref[...]

    return run(scalars, body, [(array.shape, array.dtype)], [array], after)[0]


def by_chip(scalars, pair, got):
    size = pair.shape[0] // 2

    def body(scalars, pair_ref, got_ref, out):
        core = scalars[CORE]
        for ref, chips in ((pair_ref, (0, 2 - core)), (got_ref, (1 + core, 3))):
            for i, chip in enumerate(chips):
                out[part(chip, size), :] = ref[pl.ds(i * size, size), :]

    return run(scalars, body, [((4 * size, pair.shape[1]), pair.dtype)], [pair, got])[0]


def scaled(scalars, owns, gots, gain):
    size, width = owns[0].shape[0] // 4, owns[0].shape[1]

    def body(scalars, *refs):
        own_refs, got_refs, (gain_ref, out, squares) = refs[: len(owns)], refs[len(owns) : 2 * len(owns)], refs[-3:]
        for side, side_refs in ((scalars[CORE], own_refs), (1 - scalars[CORE], got_refs)):
            for at in range(0, 4 * size, 16):
                start = (2 * (at // size) + side) * size + at % size
                rows = pl.ds(pl.multiple_of(start, 16), 16)
                total = 0.0
                for i, ref in enumerate(side_refs):
                    wide = ref[pl.ds(at, 16), :].astype(F32)
                    columns = pl.ds(i * width, width)
                    out[rows, columns] = (wide * gain_ref[:, columns]).astype(BF16)
                    total += jnp.sum(wide * wide, axis=1, keepdims=True)
                squares[rows, :] = jnp.broadcast_to(total, (16, 128))

    outs = [((8 * size, width * len(owns)), BF16), ((8 * size, 128), F32)]
    return run(scalars, body, outs, [*owns, *gots, gain])


def row_scale(scalars, squares, more_squares, after):
    def body(scalars, squares_ref, more_ref, out):
        out[...] = lax.rsqrt((squares_ref[...] + more_ref[...]) / D + 1e-05)

    return run(scalars, body, [(squares.shape, F32)], [squares, more_squares], after)[0]


def row_stats(scalars, kepts, gots, scale, gold, first, columns, before=None, after=None):
    many, rows = len(kepts), kepts[0].shape[0]
    others = [] if before is None else [before]

    def body(scalars, *refs):
        scale_ref, gold_ref, *before_refs, out = refs[2 * many :]
        blocks = []
        for at in range(0, rows, 32):
            block = pl.ds(at, 32)
            start, chunks = first, []
            for kept, got in zip(refs[:many], refs[many : 2 * many]):
                logits = (kept[block, :].astype(F32) + got[block, :].astype(F32)) * scale_ref[block, :1]
                column = lax.broadcasted_iota(jnp.int32, logits.shape, 1) + start
                chunks.append((jnp.where(column < columns, logits, -jnp.inf), column))
                start += logits.shape[1]
            tops = [jnp.max(logits, axis=1, keepdims=True) for logits, _ in chunks]
            tops += [ref[block, 0:1] for ref in before_refs]
            top = functools.reduce(jnp.maximum, tops)
            total, picked = 0.0, 0.0
            for logits, column in chunks:
                total += jnp.sum(jnp.exp(logits - top), axis=1, keepdims=True)
                hit = (column + scalars[OFFSET] == gold_ref[block, :]) & (column < columns)
                picked += jnp.sum(jnp.where(hit, logits, 0.0), axis=1, keepdims=True)
            for ref in before_refs:
                total += ref[block, 1:2] * jnp.exp(ref[block, 0:1] - top)
                picked += ref[block, 2:3]
            lane = lax.broadcasted_iota(jnp.int32, (32, 128), 1)
            blocks.append(jnp.where(lane == 0, top, jnp.where(lane == 1, total, picked)))
        blocks = jnp.concatenate(blocks)
        out[...] = blocks if before is None else blocks.T[:8]

    outs = [((rows, 128) if before is None else (8, rows), F32)]
    return run(scalars, body, outs, [*kepts, *gots, scale, gold, *others], after)[0]


def swapper(n_dm, n_hv, on_dm, flip_of):
    pairs = []
    for dm in range(n_dm):
        for hv in range(n_hv):
            flip = flip_of(hv)
            to = (dm ^ flip, hv) if on_dm else (dm, hv ^ flip)
            pairs.append((dm * n_hv + hv, to[0] * n_hv + to[1]))
    return lambda array: lax.ppermute(array, ("dm", "hv"), pairs)


def on_blocks(
    tokens, gate_weight, up_weight, down_weight, norm_gain, unembed, gold_ids, option_lengths, *, n_dm, n_hv
):
    dm, hv = lax.axis_index("dm"), lax.axis_index("hv")
    core, chip = hv & 1, hv >> 1
    dm_first, dm_last = (dm >> core) & 1, (dm >> (1 - core)) & 1
    scalars = jnp.stack([dm_first, dm_last, core, hv * unembed.shape[1]]).astype(jnp.int32)
    z_first, z_last = (swapper(n_dm, n_hv, True, flip) for flip in (lambda hv: 1 << (hv & 1), lambda hv: 2 >> (hv & 1)))
    cores, x, y, xy_first, xy_last = (
        swapper(n_dm, n_hv, False, flip)
        for flip in (lambda hv: 1, lambda hv: 2, lambda hv: 4, lambda hv: 2 << (hv & 1), lambda hv: 4 >> (hv & 1))
    )
    gain = norm_gain[None, :]
    chip_rows = 2 * tokens.shape[0]

    def sums(piece, bit=DM_FIRST):
        both = [jnp.dot(piece, weight, preferred_element_type=F32).astype(BF16) for weight in (gate_weight, up_weight)]
        return both, pick(scalars, bit, both)

    tokens = jnp.where(dm < n_dm, tokens, 0)
    from_core, from_x, from_y = cores(tokens), x(tokens), y(tokens)
    both_0, sent_0 = sums(join(scalars, CORE, [(tokens, from_core)]))
    got_0 = z_first(sent_0)
    beside, chosen = stack(scalars, from_x, from_y, sent_0)
    across = xy_last(chosen)
    both_1, sent_1 = sums(join_chips(scalars, beside, cores(beside)), DM_LAST)
    got_1 = z_last(sent_1)
    half_0 = add_half(scalars, DM_FIRST, both_0, got_0, sent_1)
    got_0 = z_last(half_0)
    across = moved(scalars, across, half_0)
    both_2, sent_2 = sums(join(scalars, CORE, [(across, cores(across))]))
    got_2 = z_first(sent_2)
    own_0 = activate(scalars, half_0, got_0, sent_2)
    got_0 = z_first(own_0)
    kept_1, sent_1 = add_split(scalars, DM_LAST, DM_FIRST, both_1, got_1, own_0)
    got_1 = z_first(sent_1)
    half_2 = add_half(scalars, DM_FIRST, both_2, got_2, kept_1)
    got_2 = z_last(half_2)
    own_1 = activate(scalars, kept_1, got_1, half_2)
    got_1 = z_first(own_1)
    whole_0 = join(scalars, DM_FIRST, [(own_0, got_0)], own_1)
    own_2 = activate(scalars, half_2, got_2, whole_0)
    got_2 = z_first(own_2)
    own_1 = join(scalars, DM_FIRST, [(own_1, got_1)], own_2)
    hidden = join_below(scalars, whole_0, [(DM_LAST, own_1, z_last(own_1)), (DM_FIRST, own_2, got_2)])
    owns, gots = [], []
    width = down_weight.shape[1] // DOWN_CHUNKS
    for at in range(0, down_weight.shape[1], width):
        ffn = jnp.dot(hidden, down_weight[:, at : at + width], preferred_element_type=F32).astype(BF16)
        stay, go = add_cores(scalars, ffn, cores(other_core(scalars, ffn)))
        stay, go = add_halves(scalars, stay, xy_first(go))
        resid = residual(scalars, tokens, at, stay, xy_last(go))
        pair, _ = stack(scalars, resid, xy_last(resid))
        owns.append(by_chip(scalars, pair, xy_first(pair)))
        gots.append(cores(owns[-1]))
    left, squares = scaled(scalars, owns, gots, gain)
    gold = lax.dynamic_slice_in_dim(gold_ids, (chip ^ (2 * dm_first + dm_last)) * chip_rows, chip_rows)[:, None]
    sent_squares = pick(scalars, DM_FIRST, [squares])
    got_squares = z_first(sent_squares)
    left = tie(left, sent_squares)
    kepts, gots, first, scale = [], [], None, None
    for at in range(0, unembed.shape[1], VOCAB_TILE):
        logits = jnp.dot(left, unembed[:, at : at + VOCAB_TILE], preferred_element_type=F32).astype(BF16)
        sent = pick(scalars, DM_FIRST, [logits])
        got = z_first(sent)
        if first is None:
            last, sent_squares = add_split(scalars, DM_FIRST, DM_LAST, [squares], got_squares, sent)
            kept_squares, got_squares = last, z_last(sent_squares)
        else:
            if scale is None:
                sent = scale = row_scale(scalars, kept_squares, got_squares, sent)
            last, sent = add_split(scalars, DM_FIRST, DM_LAST, *first, sent)
            kepts.append(last)
            gots.append(z_last(sent))
        first = ([logits], got)
        if at + VOCAB_TILE < unembed.shape[1]:
            left = tie(left, last)
    last, sent = add_split(scalars, DM_FIRST, DM_LAST, *first, last)
    columns = unembed.shape[1]
    stats = row_stats(scalars, kepts, gots, scale, gold, 0, columns, None, last)
    stats = row_stats(scalars, [last], [z_last(sent)], scale, gold, VOCAB_TILE * len(kepts), columns, stats)
    stats = stats[None]
    for bit, swap in ((dm_last, z_last), (dm_first, z_first)):
        got = swap(stats)
        stats = jnp.concatenate([jnp.where(bit == 0, stats, got), jnp.where(bit == 0, got, stats)])
    stats = stats.reshape(2, 2, 8, chip_rows)
    stats = jnp.where(chip & 1 == 0, stats, stats[:, ::-1])
    stats = jnp.where(chip >> 1 == 0, stats, stats[::-1])
    stats = lax.all_gather(stats.reshape(4, 8, chip_rows), "hv", axis=0)
    top = jnp.max(stats[:, :, 0], axis=0)
    total = jnp.sum(stats[:, :, 1] * jnp.exp(stats[:, :, 0] - top), axis=0)
    return (jnp.sum(stats[:, :, 2], axis=0) - top - jnp.log(total)).reshape(-1)


def on_any_mesh(
    tokens, gate_weight, up_weight, down_weight, norm_gain, unembed, gold_ids, option_lengths, *, n_dm, n_hv
):
    piece = lax.all_gather(tokens, "hv", axis=0, tiled=True)
    gate, up = (
        lax.psum_scatter(
            jnp.dot(piece, weight, preferred_element_type=F32), "dm", scatter_dimension=0, tiled=True
        )
        for weight in (gate_weight, up_weight)
    )
    hidden = lax.all_gather((jax.nn.silu(gate) * up).astype(BF16), "dm", axis=0, tiled=True)
    ffn = jnp.dot(hidden, down_weight, preferred_element_type=F32)
    ffn = lax.psum_scatter(ffn, "hv", scatter_dimension=0, tiled=True)
    resid = (tokens.astype(F32) + ffn).astype(BF16)
    wide = resid.astype(F32)
    squares = lax.psum(jnp.sum(wide * wide, axis=1), "dm")
    normed = (wide * lax.rsqrt(squares[:, None] / D + 1e-05) * norm_gain).astype(BF16)
    normed = lax.all_gather(normed, "hv", axis=0, tiled=True)
    logits = jnp.dot(normed, unembed, preferred_element_type=F32)
    logits = lax.psum_scatter(logits, "dm", scatter_dimension=0, tiled=True)
    rows = logits.shape[0]
    gold = lax.dynamic_slice_in_dim(gold_ids, lax.axis_index("dm") * rows, rows)
    hit = lax.broadcasted_iota(jnp.int32, logits.shape, 1) + lax.axis_index("hv") * unembed.shape[1] == gold[:, None]
    top = lax.pmax(jnp.max(logits, axis=1), "hv")
    total, gold = lax.psum(
        (jnp.sum(jnp.exp(logits - top[:, None]), axis=1), jnp.sum(jnp.where(hit, logits, 0.0), axis=1)), "hv"
    )
    return lax.all_gather(gold - top - jnp.log(total), "dm", axis=0, tiled=True)


def per_device(*args, n_dm, n_hv):
    rows = on_blocks if (n_dm, n_hv) == (4, 8) else on_any_mesh
    token_logprob = rows(*args, n_dm=n_dm, n_hv=n_hv)
    option_lengths = args[-1]
    ends = jnp.cumsum(option_lengths)
    starts = ends - option_lengths
    places = jnp.arange(token_logprob.shape[0], dtype=jnp.int32)
    member = ((places[None, :] >= starts[:, None]) & (places[None, :] < ends[:, None])).astype(F32)
    option_sums = jnp.dot(member, token_logprob, precision=lax.Precision.HIGHEST)
    option_score = option_sums / option_lengths.astype(F32)
    return (token_logprob, option_score)


def solution(mesh):
    placed = (
        P("hv", "dm"),
        P("dm", "hv"),
        P("dm", "hv"),
        P("hv", "dm"),
        P("dm"),
        P("dm", "hv"),
        P(),
        P(),
    )
    body = functools.partial(per_device, n_dm=mesh.shape["dm"], n_hv=mesh.shape["hv"])
    return jax.shard_map(
        body, mesh=mesh, in_specs=placed, out_specs=(P(), P()), check_vma=False
    )
```

```python
import functools

import jax
import jax.numpy as jnp
from jax import lax
from jax.experimental import pallas as pl
from jax.experimental.pallas import tpu as pltpu
from jax.sharding import PartitionSpec as P

D = 16384
DOWN_CHUNKS = 2
VOCAB_TILE = 1024
F32 = jnp.float32
BF16 = jnp.bfloat16
MIB = 1 << 20
VMEM = pl.BlockSpec(memory_space=pltpu.VMEM)
SMEM = pl.BlockSpec(memory_space=pltpu.SMEM)
ANY = pl.BlockSpec(memory_space=pl.ANY)
DM_FIRST, DM_LAST, CORE, OFFSET = range(4)


def run(scalars, body, outs, arrays, after=None):
    ahead = [] if after is None else [after]

    def kernel(scalars, *refs):
        body(scalars, *refs[: len(arrays)], *refs[len(arrays) + len(ahead) :])

    return pl.pallas_call(
        kernel,
        out_shape=[jax.ShapeDtypeStruct(*out) for out in outs],
        in_specs=[SMEM, *[VMEM] * len(arrays), *[ANY] * len(ahead)],
        out_specs=[VMEM] * len(outs),
        compiler_params=pltpu.CompilerParams(vmem_limit_bytes=12 * MIB),
        cost_estimate=pl.CostEstimate(
            flops=0, bytes_accessed=2 * sum(a.size * a.dtype.itemsize for a in arrays), transcendentals=0
        ),
    )(scalars, *arrays, *ahead)


def tie(array, after):
    def body(array_ref, after_ref, out):
        pass

    return pl.pallas_call(
        body,
        out_shape=jax.ShapeDtypeStruct(array.shape, array.dtype),
        in_specs=[VMEM, ANY],
        out_specs=VMEM,
        input_output_aliases={0: 0},
        compiler_params=pltpu.CompilerParams(vmem_limit_bytes=12 * MIB),
    )(array, after)


def part(which, size):
    return pl.ds(pl.multiple_of(which * size, size), size)


def add(one, two, dtype):
    return (one.astype(F32) + two.astype(F32)).astype(dtype)


def columns_of(refs, rows):
    at = 0
    for ref in refs:
        yield at, ref[rows, :]
        at += ref.shape[1]


def pick(scalars, bit, arrays, after=None):
    size = arrays[0].shape[0] // 2
    width = pl.cdiv(sum(a.shape[1] for a in arrays), 128) * 128

    def body(scalars, *refs):
        for at, values in columns_of(refs[:-1], part(1 - scalars[bit], size)):
            refs[-1][:, pl.ds(at, values.shape[1])] = values

    return run(scalars, body, [((size, width), arrays[0].dtype)], arrays, after)[0]


def add_split(scalars, before, bit, arrays, got, after=None):
    def body(scalars, *refs):
        which = scalars[bit]
        size = got.shape[0] // 2
        for out, side in ((refs[-2], which), (refs[-1], 1 - which)):
            start = pl.multiple_of((2 * scalars[before] + side) * size, size)
            for at, values in columns_of(refs[: len(arrays)], pl.ds(start, size)):
                columns = pl.ds(at, values.shape[1])
                out[:, columns] = add(values, refs[len(arrays)][part(side, size), columns], out.dtype)

    return run(scalars, body, [((got.shape[0] // 2, got.shape[1]), got.dtype)] * 2, [*arrays, got], after)


def add_half(scalars, before, arrays, got, after=None):
    def body(scalars, *refs):
        size = got.shape[0]
        for at, values in columns_of(refs[: len(arrays)], part(scalars[before], size)):
            columns = pl.ds(at, values.shape[1])
            refs[-1][:, columns] = add(values, refs[len(arrays)][:, columns], got.dtype)

    return run(scalars, body, [(got.shape, got.dtype)], [*arrays, got], after)[0]


def join(scalars, bit, pairs, after=None):
    rows = sum(2 * own.shape[0] for own, _ in pairs)

    def body(scalars, *refs):
        which, at = scalars[bit], 0
        for i, (own, _) in enumerate(pairs):
            size = own.shape[0]
            for place, ref in ((which, refs[2 * i]), (1 - which, refs[2 * i + 1])):
                refs[-1][pl.ds(pl.multiple_of(at + place * size, 16), size), :] = ref[...]
            at += 2 * size

    own = pairs[0][0]
    return run(scalars, body, [((rows, own.shape[1]), own.dtype)], [a for pair in pairs for a in pair], after)[0]


def join_below(scalars, above, pairs):
    rows = above.shape[0] + sum(2 * own.shape[0] for _, own, _ in pairs)

    def body(scalars, above_ref, *refs):
        refs[-1][pl.ds(0, above.shape[0]), :] = above_ref[...]
        at = above.shape[0]
        for i, (bit, own, _) in enumerate(pairs):
            which, size = scalars[bit], own.shape[0]
            for place, ref in ((which, refs[2 * i]), (1 - which, refs[2 * i + 1])):
                refs[-1][pl.ds(pl.multiple_of(at + place * size, 16), size), :] = ref[...]
            at += 2 * size

    arrays = [above, *[array for _, *pair in pairs for array in pair]]
    return run(scalars, body, [((rows, above.shape[1]), above.dtype)], arrays)[0]


def join_chips(scalars, own, got):
    size = own.shape[0] // 2

    def body(scalars, own_ref, got_ref, out):
        for side, ref in ((scalars[CORE], own_ref), (1 - scalars[CORE], got_ref)):
            for chip in range(2):
                rows = pl.ds(pl.multiple_of((2 * chip + side) * size, size), size)
                out[rows, :] = ref[pl.ds(chip * size, size), :]

    return run(scalars, body, [((4 * size, own.shape[1]), own.dtype)], [own, got])[0]


def activate(scalars, kept, got, after=None):
    def body(scalars, kept_ref, got_ref, out):
        width = out.shape[1]
        gate, up = (
            kept_ref[:, pl.ds(at, width)].astype(F32) + got_ref[:, pl.ds(at, width)].astype(F32) for at in (0, width)
        )
        out[...] = (gate / (1.0 + jnp.exp(-gate)) * up).astype(BF16)

    return run(scalars, body, [((kept.shape[0], kept.shape[1] // 2), BF16)], [kept, got], after)[0]


def other_core(scalars, ffn):
    size = ffn.shape[0] // 8

    def body(scalars, ref, out):
        for chip in range(4):
            start = pl.multiple_of((2 * chip + 1 - scalars[CORE]) * size, size)
            out[pl.ds(chip * size, size), :] = ref[pl.ds(start, size), :]

    return run(scalars, body, [((4 * size, ffn.shape[1]), ffn.dtype)], [ffn])[0]


def add_cores(scalars, ffn, got):
    size = ffn.shape[0] // 8

    def body(scalars, ref, got_ref, stay, go):
        core = scalars[CORE]
        for out, chips in ((stay, (0, 2 - core)), (go, (1 + core, 3))):
            for i, chip in enumerate(chips):
                rows = pl.ds(pl.multiple_of((2 * chip + core) * size, size), size)
                out[pl.ds(i * size, size), :] = add(ref[rows, :], got_ref[part(chip, size), :], out.dtype)

    return run(scalars, body, [((2 * size, ffn.shape[1]), ffn.dtype)] * 2, [ffn, got])


def add_halves(scalars, stay, got):
    size = stay.shape[0] // 2

    def body(scalars, stay_ref, got_ref, first, second):
        for at, out in ((0, first), (size, second)):
            rows = pl.ds(at, size)
            out[...] = add(stay_ref[rows, :], got_ref[rows, :], out.dtype)

    return run(scalars, body, [((size, stay.shape[1]), stay.dtype)] * 2, [stay, got])


def residual(scalars, mine, at, kept, got):
    width = kept.shape[1]

    def body(scalars, mine_ref, kept_ref, got_ref, out):
        ffn = kept_ref[...].astype(F32) + got_ref[...].astype(F32)
        out[...] = (mine_ref[:, pl.ds(at, width)].astype(F32) + ffn).astype(BF16)

    return run(scalars, body, [(kept.shape, BF16)], [mine, kept, got])[0]


def stack(scalars, first, second, after=None):
    size = first.shape[0]

    def body(scalars, first_ref, second_ref, out, chosen):
        out[pl.ds(0, size), :] = first_ref[...]
        out[pl.ds(size, size), :] = second_ref[...]
        if after is not None:
            chosen[...] = jnp.where(scalars[CORE] == 0, first_ref[...], second_ref[...])

    outs = [((2 * size, first.shape[1]), first.dtype), (first.shape if after is not None else (16, 128), first.dtype)]
    return run(scalars, body, outs, [first, second], after)


def moved(scalars, array, after):
    def body(scalars, ref, out):
        out[...] = ref[...]

    return run(scalars, body, [(array.shape, array.dtype)], [array], after)[0]


def by_chip(scalars, pair, got):
    size = pair.shape[0] // 2

    def body(scalars, pair_ref, got_ref, out):
        core = scalars[CORE]
        for ref, chips in ((pair_ref, (0, 2 - core)), (got_ref, (1 + core, 3))):
            for i, chip in enumerate(chips):
                out[part(chip, size), :] = ref[pl.ds(i * size, size), :]

    return run(scalars, body, [((4 * size, pair.shape[1]), pair.dtype)], [pair, got])[0]


def scaled(scalars, owns, gots, gain):
    size, width = owns[0].shape[0] // 4, owns[0].shape[1]

    def body(scalars, *refs):
        own_refs, got_refs, (gain_ref, out, squares) = refs[: len(owns)], refs[len(owns) : 2 * len(owns)], refs[-3:]
        for side, side_refs in ((scalars[CORE], own_refs), (1 - scalars[CORE], got_refs)):
            for at in range(0, 4 * size, 16):
                start = (2 * (at // size) + side) * size + at % size
                rows = pl.ds(pl.multiple_of(start, 16), 16)
                total = 0.0
                for i, ref in enumerate(side_refs):
                    wide = ref[pl.ds(at, 16), :].astype(F32)
                    columns = pl.ds(i * width, width)
                    out[rows, columns] = (wide * gain_ref[:, columns]).astype(BF16)
                    total += jnp.sum(wide * wide, axis=1, keepdims=True)
                squares[rows, :] = jnp.broadcast_to(total, (16, 128))

    outs = [((8 * size, width * len(owns)), BF16), ((8 * size, 128), F32)]
    return run(scalars, body, outs, [*owns, *gots, gain])


def row_scale(scalars, squares, more_squares, after):
    def body(scalars, squares_ref, more_ref, out):
        out[...] = lax.rsqrt((squares_ref[...] + more_ref[...]) / D + 1e-05)

    return run(scalars, body, [(squares.shape, F32)], [squares, more_squares], after)[0]


def row_stats(scalars, kepts, gots, scale, gold, first, columns, before=None, after=None):
    many, rows = len(kepts), kepts[0].shape[0]
    others = [] if before is None else [before]

    def body(scalars, *refs):
        scale_ref, gold_ref, *before_refs, out = refs[2 * many :]
        blocks = []
        for at in range(0, rows, 32):
            block = pl.ds(at, 32)
            start, chunks = first, []
            for kept, got in zip(refs[:many], refs[many : 2 * many]):
                logits = (kept[block, :].astype(F32) + got[block, :].astype(F32)) * scale_ref[block, :1]
                column = lax.broadcasted_iota(jnp.int32, logits.shape, 1) + start
                chunks.append((jnp.where(column < columns, logits, -jnp.inf), column))
                start += logits.shape[1]
            tops = [jnp.max(logits, axis=1, keepdims=True) for logits, _ in chunks]
            tops += [ref[block, 0:1] for ref in before_refs]
            top = functools.reduce(jnp.maximum, tops)
            total, picked = 0.0, 0.0
            for logits, column in chunks:
                total += jnp.sum(jnp.exp(logits - top), axis=1, keepdims=True)
                hit = (column + scalars[OFFSET] == gold_ref[block, :]) & (column < columns)
                picked += jnp.sum(jnp.where(hit, logits, 0.0), axis=1, keepdims=True)
            for ref in before_refs:
                total += ref[block, 1:2] * jnp.exp(ref[block, 0:1] - top)
                picked += ref[block, 2:3]
            lane = lax.broadcasted_iota(jnp.int32, (32, 128), 1)
            blocks.append(jnp.where(lane == 0, top, jnp.where(lane == 1, total, picked)))
        blocks = jnp.concatenate(blocks)
        out[...] = blocks if before is None else blocks.T[:8]

    outs = [((rows, 128) if before is None else (8, rows), F32)]
    return run(scalars, body, outs, [*kepts, *gots, scale, gold, *others], after)[0]


def swapper(n_dm, n_hv, on_dm, flip_of):
    pairs = []
    for dm in range(n_dm):
        for hv in range(n_hv):
            flip = flip_of(hv)
            to = (dm ^ flip, hv) if on_dm else (dm, hv ^ flip)
            pairs.append((dm * n_hv + hv, to[0] * n_hv + to[1]))
    return lambda array: lax.ppermute(array, ("dm", "hv"), pairs)


def on_blocks(
    tokens, gate_weight, up_weight, down_weight, norm_gain, unembed, gold_ids, option_lengths, *, n_dm, n_hv
):
    dm, hv = lax.axis_index("dm"), lax.axis_index("hv")
    core, chip = hv & 1, hv >> 1
    dm_first, dm_last = (dm >> core) & 1, (dm >> (1 - core)) & 1
    scalars = jnp.stack([dm_first, dm_last, core, hv * unembed.shape[1]]).astype(jnp.int32)
    z_first, z_last = (swapper(n_dm, n_hv, True, flip) for flip in (lambda hv: 1 << (hv & 1), lambda hv: 2 >> (hv & 1)))
    cores, x, y, xy_first, xy_last = (
        swapper(n_dm, n_hv, False, flip)
        for flip in (lambda hv: 1, lambda hv: 2, lambda hv: 4, lambda hv: 2 << (hv & 1), lambda hv: 4 >> (hv & 1))
    )
    gain = norm_gain[None, :]
    chip_rows = 2 * tokens.shape[0]

    def sums(piece, bit=DM_FIRST):
        both = [jnp.dot(piece, weight, preferred_element_type=F32).astype(BF16) for weight in (gate_weight, up_weight)]
        return both, pick(scalars, bit, both)

    tokens = jnp.where(dm < n_dm, tokens, 0)
    from_core, from_x, from_y = cores(tokens), x(tokens), y(tokens)
    both_0, sent_0 = sums(join(scalars, CORE, [(tokens, from_core)]))
    got_0 = z_first(sent_0)
    beside, chosen = stack(scalars, from_x, from_y, sent_0)
    across = xy_last(chosen)
    both_1, sent_1 = sums(join_chips(scalars, beside, cores(beside)), DM_LAST)
    got_1 = z_last(sent_1)
    half_0 = add_half(scalars, DM_FIRST, both_0, got_0, sent_1)
    got_0 = z_last(half_0)
    across = moved(scalars, across, half_0)
    both_2, sent_2 = sums(join(scalars, CORE, [(across, cores(across))]))
    got_2 = z_first(sent_2)
    own_0 = activate(scalars, half_0, got_0, sent_2)
    got_0 = z_first(own_0)
    kept_1, sent_1 = add_split(scalars, DM_LAST, DM_FIRST, both_1, got_1, own_0)
    got_1 = z_first(sent_1)
    half_2 = add_half(scalars, DM_FIRST, both_2, got_2, kept_1)
    got_2 = z_last(half_2)
    own_1 = activate(scalars, kept_1, got_1, half_2)
    got_1 = z_first(own_1)
    whole_0 = join(scalars, DM_FIRST, [(own_0, got_0)], own_1)
    own_2 = activate(scalars, half_2, got_2, whole_0)
    got_2 = z_first(own_2)
    own_1 = join(scalars, DM_FIRST, [(own_1, got_1)], own_2)
    hidden = join_below(scalars, whole_0, [(DM_LAST, own_1, z_last(own_1)), (DM_FIRST, own_2, got_2)])
    owns, gots = [], []
    width = down_weight.shape[1] // DOWN_CHUNKS
    for at in range(0, down_weight.shape[1], width):
        ffn = jnp.dot(hidden, down_weight[:, at : at + width], preferred_element_type=F32).astype(BF16)
        stay, go = add_cores(scalars, ffn, cores(other_core(scalars, ffn)))
        stay, go = add_halves(scalars, stay, xy_first(go))
        resid = residual(scalars, tokens, at, stay, xy_last(go))
        pair, _ = stack(scalars, resid, xy_last(resid))
        owns.append(by_chip(scalars, pair, xy_first(pair)))
        gots.append(cores(owns[-1]))
    left, squares = scaled(scalars, owns, gots, gain)
    gold = lax.dynamic_slice_in_dim(gold_ids, (chip ^ (2 * dm_first + dm_last)) * chip_rows, chip_rows)[:, None]
    sent_squares = pick(scalars, DM_FIRST, [squares])
    got_squares = z_first(sent_squares)
    left = tie(left, sent_squares)
    kepts, gots, first, scale = [], [], None, None
    for at in range(0, unembed.shape[1], VOCAB_TILE):
        logits = jnp.dot(left, unembed[:, at : at + VOCAB_TILE], preferred_element_type=F32).astype(BF16)
        sent = pick(scalars, DM_FIRST, [logits])
        got = z_first(sent)
        if first is None:
            last, sent_squares = add_split(scalars, DM_FIRST, DM_LAST, [squares], got_squares, sent)
            kept_squares, got_squares = last, z_last(sent_squares)
        else:
            if scale is None:
                sent = scale = row_scale(scalars, kept_squares, got_squares, sent)
            last, sent = add_split(scalars, DM_FIRST, DM_LAST, *first, sent)
            kepts.append(last)
            gots.append(z_last(sent))
        first = ([logits], got)
        if at + VOCAB_TILE < unembed.shape[1]:
            left = tie(left, last)
    last, sent = add_split(scalars, DM_FIRST, DM_LAST, *first, last)
    columns = unembed.shape[1]
    stats = row_stats(scalars, kepts, gots, scale, gold, 0, columns, None, last)
    stats = row_stats(scalars, [last], [z_last(sent)], scale, gold, VOCAB_TILE * len(kepts), columns, stats)
    def ordered(bit, own, got):
        return jnp.concatenate([jnp.where(bit == 0, own, got), jnp.where(bit == 0, got, own)])

    stats = stats[None]
    beside, across, opposite = z_last(stats), z_first(stats), swapper(n_dm, n_hv, True, lambda hv: 3)(stats)
    stats = ordered(dm_first, ordered(dm_last, stats, beside), ordered(dm_last, across, opposite))
    stats = stats.reshape(2, 2, 8, chip_rows)
    stats = jnp.where(chip & 1 == 0, stats, stats[:, ::-1])
    stats = jnp.where(chip >> 1 == 0, stats, stats[::-1])
    stats = lax.all_gather(stats.reshape(4, 8, chip_rows), "hv", axis=0)
    top = jnp.max(stats[:, :, 0], axis=0)
    total = jnp.sum(stats[:, :, 1] * jnp.exp(stats[:, :, 0] - top), axis=0)
    return (jnp.sum(stats[:, :, 2], axis=0) - top - jnp.log(total)).reshape(-1)


def on_any_mesh(
    tokens, gate_weight, up_weight, down_weight, norm_gain, unembed, gold_ids, option_lengths, *, n_dm, n_hv
):
    piece = lax.all_gather(tokens, "hv", axis=0, tiled=True)
    gate, up = (
        lax.psum_scatter(
            jnp.dot(piece, weight, preferred_element_type=F32), "dm", scatter_dimension=0, tiled=True
        )
        for weight in (gate_weight, up_weight)
    )
    hidden = lax.all_gather((jax.nn.silu(gate) * up).astype(BF16), "dm", axis=0, tiled=True)
    ffn = jnp.dot(hidden, down_weight, preferred_element_type=F32)
    ffn = lax.psum_scatter(ffn, "hv", scatter_dimension=0, tiled=True)
    resid = (tokens.astype(F32) + ffn).astype(BF16)
    wide = resid.astype(F32)
    squares = lax.psum(jnp.sum(wide * wide, axis=1), "dm")
    normed = (wide * lax.rsqrt(squares[:, None] / D + 1e-05) * norm_gain).astype(BF16)
    normed = lax.all_gather(normed, "hv", axis=0, tiled=True)
    logits = jnp.dot(normed, unembed, preferred_element_type=F32)
    logits = lax.psum_scatter(logits, "dm", scatter_dimension=0, tiled=True)
    rows = logits.shape[0]
    gold = lax.dynamic_slice_in_dim(gold_ids, lax.axis_index("dm") * rows, rows)
    hit = lax.broadcasted_iota(jnp.int32, logits.shape, 1) + lax.axis_index("hv") * unembed.shape[1] == gold[:, None]
    top = lax.pmax(jnp.max(logits, axis=1), "hv")
    total, gold = lax.psum(
        (jnp.sum(jnp.exp(logits - top[:, None]), axis=1), jnp.sum(jnp.where(hit, logits, 0.0), axis=1)), "hv"
    )
    return lax.all_gather(gold - top - jnp.log(total), "dm", axis=0, tiled=True)


def per_device(*args, n_dm, n_hv):
    rows = on_blocks if (n_dm, n_hv) == (4, 8) else on_any_mesh
    token_logprob = rows(*args, n_dm=n_dm, n_hv=n_hv)
    option_lengths = args[-1]
    ends = jnp.cumsum(option_lengths)
    starts = ends - option_lengths
    places = jnp.arange(token_logprob.shape[0], dtype=jnp.int32)
    member = ((places[None, :] >= starts[:, None]) & (places[None, :] < ends[:, None])).astype(F32)
    option_sums = jnp.dot(member, token_logprob, precision=lax.Precision.HIGHEST)
    option_score = option_sums / option_lengths.astype(F32)
    return (token_logprob, option_score)


def solution(mesh):
    placed = (
        P("hv", "dm"),
        P("dm", "hv"),
        P("dm", "hv"),
        P("hv", "dm"),
        P("dm"),
        P("dm", "hv"),
        P(),
        P(),
    )
    body = functools.partial(per_device, n_dm=mesh.shape["dm"], n_hv=mesh.shape["hv"])
    return jax.shard_map(
        body, mesh=mesh, in_specs=placed, out_specs=(P(), P()), check_vma=False
    )
```
